32 devices in a mesh: row: 4 (over y, x), col: 8 (over z, core).
Axes of the slice: x: 2, y: 2, z: 4, core: 2. Of those that a mesh axis runs over, the one named last changes fastest.
Arguments:
- feats: bfloat16 [8, 512, 512], P('col', 'row'), may hold values from -6 to 6
- weight: bfloat16 [512, 512], replicated, may hold values from -0.25 to 0.25
- cotangent: bfloat16 [4, 1024, 512], P('row', 'col'), may hold values from -6 to 6
- tile_values: bfloat16 [4, 8, 24, 128, 128], P('row', 'col'), may hold values from -0.15625 to 0.15625
- tile_rows: int32 [4, 8, 24], P('row', 'col'), may hold values from 0 to 7, as said below
- tile_cols: int32 [4, 8, 24], P('row', 'col'), may hold values from 0 to 3, as said below
- tile_count: int32 [4, 8], P('row', 'col'), may hold values from 1 to 24, as said below
Outputs:
- layer_out: bfloat16 [4, 1024, 512], P('row', 'col')
- feat_grad: bfloat16 [8, 512, 512], P('col', 'row')
- weight_grad: float32 [512, 512], replicated
The draws below stay inside these ranges and needn't reach their ends.
Inputs may be any that keep to these rules, and one draw needn't show every extreme that they name: `tile_rows`: with tile_cols, the tile coordinates of each block's listed tiles; no tile appears twice in a block's list. `tile_cols`: with tile_rows, the tile coordinates of each block's listed tiles. `tile_count`: slots at or beyond a block's count are unused; some block lists exactly 24 tiles.
All inputs are finite; a program needn't handle non-finite values.
Results may differ from the reference program's by a relative error of at most 0.024.
Values may be sent and summed in bfloat16 or wider, within the bound.
No kernel may reach another device: no remote copies, remote signals or barrier semaphores. Data moves between devices by JAX's collectives and lax.ppermute only.
A program may use at most 128 MiB of HBM per device.

```python
import jax
import jax.numpy as jnp
from jax import lax

F = 512
TILE = 128
NODES = 4096
ROW_PANEL = 1024
COL_PANEL = 512
ROW_TILES = 8
COL_TILES = 4
TILE_SLOTS = 24
N_ROW = 4
N_COL = 8


def tile_layout(key):
    block_keys = jax.random.split(jax.random.fold_in(key, 11), N_ROW * N_COL)

    def one_block(block_key):
        return jax.random.permutation(block_key, ROW_TILES * COL_TILES)[:TILE_SLOTS]
    chosen = jax.vmap(one_block)(block_keys).astype(jnp.int32)
    return chosen.reshape(N_ROW, N_COL, TILE_SLOTS)


def draw_tile_rows(key, part):
    return (tile_layout(key) // COL_TILES).astype(jnp.int32)


def draw_tile_cols(key, part):
    return (tile_layout(key) % COL_TILES).astype(jnp.int32)


def draw_tile_count(key, part):
    halvings = jax.random.randint(jax.random.fold_in(key, 13), (N_ROW * N_COL,), 0, 4).astype(jnp.int32)
    divisor = jnp.left_shift(jnp.ones_like(halvings), halvings)
    counted = jnp.maximum(TILE_SLOTS // divisor, 1).astype(jnp.int32)
    forced = jax.random.randint(jax.random.fold_in(key, 17), (), 0, N_ROW * N_COL)
    counted = counted.at[forced].set(TILE_SLOTS)
    return counted.reshape(N_ROW, N_COL).astype(jnp.int32)


def steps_of(key, dims, shards, low, largest):
    level = 1.0
    for axis_at, shards_of in shards:
        draws = jax.random.uniform(jax.random.fold_in(jax.random.fold_in(key, 6), axis_at), (shards_of,), jnp.float32, low / len(shards), largest / len(shards))
        level = level * jnp.repeat(jnp.exp(draws), dims[axis_at] // shards_of).reshape((-1,) + (1,) * (len(dims) - 1 - axis_at))
    return level


def scatter_about(stream_key, shape, scale, limit, pieces=(), held_as=jnp.bfloat16):
    entries = jax.random.normal(stream_key, shape, jnp.float32) * scale
    if len(pieces) > 0:
        entries = steps_of(stream_key, shape, pieces, -0.22, 0.18) * entries
    return jnp.clip(entries, min=-limit, max=limit).astype(held_as)


def setup_inputs(seed: int = 0) -> dict:
    streams_of = jax.random.split(jax.random.key(seed), 8)
    return {
        "feats": scatter_about(streams_of[0], (N_COL, COL_PANEL, F), 1.0, 6.0, ((0, 8), (1, 4))),
        "weight": scatter_about(streams_of[1], (F, F), F ** -0.5, 0.25),
        "cotangent": scatter_about(streams_of[2], (N_ROW, ROW_PANEL, F), 1.0, 6.0, ((0, 4), (1, 8))),
        "tile_values": scatter_about(streams_of[3], (N_ROW, N_COL, TILE_SLOTS, TILE, TILE), (TILE_SLOTS * N_COL * 128 // (2 * ROW_TILES)) ** -0.5, 0.15625, ((0, 4), (1, 8))),
        "tile_rows": draw_tile_rows(jax.random.fold_in(streams_of[7], 71), 0),
        "tile_cols": draw_tile_cols(jax.random.fold_in(streams_of[7], 71), 0),
        "tile_count": draw_tile_count(jax.random.fold_in(streams_of[7], 71), 0),
    }


def reference(feats, weight, cotangent, tile_values, tile_rows, tile_cols, tile_count):
    feature_width = feats.shape[2]
    panels = feats.reshape(N_COL, COL_TILES, 128, feature_width)
    slot_ids = jnp.arange(TILE_SLOTS, dtype=jnp.int32)
    block_ids = jnp.arange(N_ROW * N_COL, dtype=jnp.int32)

    def forward_block(running, block_index):
        block_row = block_index // N_COL
        block_col = block_index % N_COL
        keep_mask = (slot_ids < tile_count[block_row, block_col]).astype(jnp.float32)
        tiles_now = tile_values[block_row, block_col].astype(jnp.float32) * keep_mask[:, None, None]
        picked = panels[block_col][tile_cols[block_row, block_col]].astype(jnp.float32)
        products = jnp.einsum("gab,gbf->gaf", tiles_now, picked)
        row_part = jnp.zeros((ROW_TILES, 128, feature_width), jnp.float32).at[tile_rows[block_row, block_col]].add(products)
        row_part = lax.optimization_barrier(row_part.astype(jnp.bfloat16)).astype(jnp.float32)
        return running.at[block_row].add(row_part), None

    start_sum = jnp.zeros((N_ROW, ROW_TILES, 128, feature_width), jnp.float32)
    summed, _ = lax.scan(forward_block, start_sum, block_ids)
    summed_bf = summed.reshape(N_ROW * ROW_TILES * 128, feature_width).astype(jnp.bfloat16)
    hidden = jnp.dot(summed_bf, weight, preferred_element_type=jnp.float32)
    sigmoid_part = jax.nn.sigmoid(hidden)
    layer_out = (hidden * sigmoid_part).astype(jnp.bfloat16).reshape(N_ROW, ROW_TILES * 128, feature_width)
    hidden_grad = (cotangent.reshape(-1, feature_width).astype(jnp.float32) * sigmoid_part * (1.0 + hidden * (1.0 - sigmoid_part))).astype(jnp.bfloat16)
    grad_rows = lax.dot_general(hidden_grad, weight, (((1,), (1,)), ((), ())), preferred_element_type=jnp.float32).astype(jnp.bfloat16)
    weight_grad = lax.dot_general(summed_bf, hidden_grad, (((0,), (0,)), ((), ())), preferred_element_type=jnp.float32) * (NODES ** -0.5)
    grad_tiles = grad_rows.reshape(N_ROW, ROW_TILES, 128, feature_width)

    def backward_block(running, block_index):
        block_row = block_index // N_COL
        block_col = block_index % N_COL
        keep_mask = (slot_ids < tile_count[block_row, block_col]).astype(jnp.float32)
        tiles_now = tile_values[block_row, block_col].astype(jnp.float32) * keep_mask[:, None, None]
        picked = grad_tiles[block_row][tile_rows[block_row, block_col]].astype(jnp.float32)
        products = jnp.einsum("gab,gaf->gbf", tiles_now, picked)
        block_part = jnp.zeros((COL_TILES, 128, feature_width), jnp.float32).at[tile_cols[block_row, block_col]].add(products)
        block_part = lax.optimization_barrier(block_part.astype(jnp.bfloat16)).astype(jnp.float32)
        return running.at[block_col].add(block_part), None

    start_grad = jnp.zeros((N_COL, COL_TILES, 128, feature_width), jnp.float32)
    grad_sum, _ = lax.scan(backward_block, start_grad, block_ids)
    feat_grad = grad_sum.reshape(N_COL, COL_TILES * 128, feature_width).astype(jnp.bfloat16)
    return layer_out, feat_grad, weight_grad
```

```python
import functools

import jax
import jax.numpy as jnp
from jax import lax
from jax.experimental import pallas as pl
from jax.experimental.pallas import tpu as pltpu
from jax.sharding import PartitionSpec as P

F32 = jnp.float32
BF16 = jnp.bfloat16
VMEM = pl.BlockSpec(memory_space=pltpu.VMEM)
SMEM = pl.BlockSpec(memory_space=pltpu.SMEM)
TILE = 128


def call(kernel, outs, args, specs=None, scratch=(), work=0):
    held = sum(a.size * a.dtype.itemsize for a in (*args, *outs))
    return pl.pallas_call(
        kernel,
        out_shape=outs,
        in_specs=specs or [VMEM] * len(args),
        out_specs=[VMEM] * len(outs),
        scratch_shapes=scratch,
        compiler_params=pltpu.CompilerParams(vmem_limit_bytes=12 * 2**20 + 3 * held),
        cost_estimate=pl.CostEstimate(flops=work, bytes_accessed=held, transcendentals=0),
    )(*args)


def like(*shape, dtype=BF16):
    return jax.ShapeDtypeStruct(shape, dtype)


def swap(value, axis, size, mask):
    return lax.ppermute(value, axis, [(i, i ^ mask) for i in range(size)])


def tree(terms):
    while len(terms) > 1:
        terms = [terms[i] + terms[i + 1] for i in range(0, len(terms), 2)]
    return terms[0]


def densify(n_z, values, rows, cols, count, dense, dense_t):
    me_row, me_col = lax.axis_index("row"), lax.axis_index("col")
    dense[...] = jnp.zeros_like(dense)
    dense_t[...] = jnp.zeros_like(dense_t)

    def place(s, carry):
        far = rows[0, 0, s] ^ me_col
        at = pl.multiple_of(((far & 1) * n_z + (far >> 1)) * TILE, TILE)
        to = pl.multiple_of((cols[0, 0, s] ^ me_row) * TILE, TILE)
        tile = values[0, 0, s]
        dense[pl.ds(at, TILE), pl.ds(to, TILE)] = tile
        dense_t[pl.ds(to, TILE), pl.ds(at, TILE)] = tile.T
        return carry

    lax.fori_loop(0, count[0, 0], place, 0)


def forward(first, dense, *refs):
    *feats, out = refs
    size = out.shape[0]
    panel = jnp.concatenate([f[...] for f in feats], axis=0)
    out[...] = jnp.dot(
        dense[first : first + size, :], panel, preferred_element_type=F32
    ).astype(out.dtype)


def add_split(mine, other, *outs):
    rows = outs[0].shape[0]
    for k, out in enumerate(outs):
        part = pl.ds(k * rows, rows)
        out[...] = (mine[part, :].astype(F32) + other[part, :].astype(F32)).astype(out.dtype)


def add_all(*refs):
    *terms, out = refs
    out[...] = tree([t[...].astype(F32) for t in terms]).astype(out.dtype)


def dense_layer(n_z, weight, cotangent, *refs):
    terms, (layer_out, summed, hidden_grad, grad_rows) = refs[:n_z], refs[n_z:]
    total = tree([t[...].astype(F32) for t in terms]).astype(BF16)
    summed[...] = total
    hidden = jnp.dot(total, weight[...], preferred_element_type=F32)
    gate = jax.nn.sigmoid(hidden)
    layer_out[...] = (hidden * gate).astype(BF16)
    grad = (cotangent[0].astype(F32) * gate * (1.0 + hidden * (1.0 - gate))).astype(BF16)
    hidden_grad[...] = grad
    grad_rows[...] = lax.dot_general(
        grad, weight[...], (((1,), (1,)), ((), ())), preferred_element_type=F32
    ).astype(BF16)


def weight_term(n_row, scale, summed, hidden_grad, mine, other, whole):
    whole[...] = (
        lax.dot_general(
            summed[...], hidden_grad[...], (((0,), (0,)), ((), ())), preferred_element_type=F32
        )
        * scale
    )
    me_row, core = lax.axis_index("row"), lax.axis_index("col") & 1
    half = mine.shape[0]
    piece = half // n_row
    for k in range(n_row):
        inside = (me_row ^ k) * piece
        part = pl.ds(k * piece, piece)
        at = pl.multiple_of(core * half + inside, piece)
        mine[part, :] = whole[pl.ds(at, piece), :]
        at = pl.multiple_of((1 - core) * half + inside, piece)
        other[part, :] = whole[pl.ds(at, piece), :].astype(BF16)


def backward(n_z, dense_t, *refs):
    grads, outs = refs[: 2 * n_z], refs[2 * n_z :]
    panel = jnp.concatenate([g[...] for g in grads], axis=0)
    total = jnp.dot(dense_t[...], panel, preferred_element_type=F32)
    for k, out in enumerate(outs):
        out[...] = total[k * TILE : (k + 1) * TILE].astype(out.dtype)


def join(*refs):
    *pieces, out = refs
    me_row = lax.axis_index("row")
    piece = pieces[0].shape[0]
    for k, ref in enumerate(pieces):
        at = pl.multiple_of((me_row ^ k) * piece, piece)
        out[pl.ds(at, piece), :] = ref[...]


def spread(mine, other, out):
    core = lax.axis_index("col") & 1
    half = mine.shape[0]
    out[pl.ds(pl.multiple_of(core * half, half), half), :] = mine[...].astype(F32)
    out[pl.ds(pl.multiple_of((1 - core) * half, half), half), :] = other[...].astype(F32)


def local(feats, weight, cotangent, tile_values, tile_rows, tile_cols, tile_count):
    width = feats.shape[2]
    n_row, n_col = lax.axis_size("row"), lax.axis_size("col")
    n_z = n_col // 2
    row_nodes, col_nodes = n_col * TILE, n_row * TILE
    half = row_nodes // 2
    row_swap = lambda x, k: swap(x, "row", n_row, k)
    z_swap = lambda x, k: swap(x, "col", n_col, 2 * k)
    core_swap = lambda x: swap(x, "col", n_col, 1)

    own = feats[0]
    panel = [own] + [row_swap(own, k) for k in range(1, n_row)]
    dense, dense_t = call(
        functools.partial(densify, n_z),
        [like(row_nodes, col_nodes), like(col_nodes, row_nodes)],
        (tile_values, tile_rows, tile_cols, tile_count),
        specs=[VMEM, SMEM, SMEM, SMEM],
    )
    work = 2 * half * col_nodes * width
    (other,) = call(functools.partial(forward, half), [like(half, width)], (dense, *panel), work=work)
    other = core_swap(other)
    (mine,) = call(
        functools.partial(forward, 0), [like(half, width, dtype=F32)], (dense, *panel), work=work
    )
    parts = call(
        add_split,
        [like(TILE, width, dtype=F32)] + [like(TILE, width)] * (n_z - 1),
        (mine, other),
    )
    terms = [parts[0]] + [z_swap(parts[k], k) for k in range(1, n_z)]
    layer_out, summed, hidden_grad, grad_rows = call(
        functools.partial(dense_layer, n_z),
        [like(TILE, width)] * 4,
        (weight, cotangent, *terms),
        work=4 * TILE * width * width,
    )
    same = [grad_rows] + [z_swap(grad_rows, k) for k in range(1, n_z)]
    cross = [core_swap(g) for g in same]

    piece = width // 2 // n_row
    mine_w, other_w = call(
        functools.partial(weight_term, n_row, (n_row * n_col * TILE) ** -0.5),
        [like(width // 2, width, dtype=F32), like(width // 2, width)],
        (summed, hidden_grad),
        scratch=[pltpu.VMEM((width, width), F32)],
        work=2 * TILE * width * width,
    )
    other_w = core_swap(other_w)
    parts_w = call(add_split, [like(piece, width)] * n_row, (mine_w, other_w))
    terms_w = [parts_w[0]] + [row_swap(parts_w[k], k) for k in range(1, n_row)]
    (plane_w,) = call(add_all, [like(piece, width)], terms_w)
    terms_w = [plane_w] + [z_swap(plane_w, k) for k in range(1, n_z)]
    (final_w,) = call(add_all, [like(piece, width)], terms_w)
    pieces_w = [final_w] + [row_swap(final_w, k) for k in range(1, n_row)]
    (half_w,) = call(join, [like(width // 2, width)], pieces_w)
    (weight_grad,) = call(spread, [like(width, width, dtype=F32)], (half_w, core_swap(half_w)))

    back = call(
        functools.partial(backward, n_z),
        [like(TILE, width, dtype=F32)] + [like(TILE, width)] * (n_row - 1),
        (dense_t, *same, *cross),
        work=2 * work,
    )
    terms = [back[0]] + [row_swap(back[k], k) for k in range(1, n_row)]
    (feat_grad,) = call(add_all, [like(TILE, width)], terms)
    return layer_out[None], feat_grad[None], weight_grad


def solution(mesh):
    in_specs = (
        P("col", "row", None),
        P(),
        P("row", "col", None),
        P("row", "col", None, None, None),
        P("row", "col", None),
        P("row", "col", None),
        P("row", "col"),
    )
    out_specs = (P("row", "col", None), P("col", "row", None), P())
    return jax.shard_map(local, mesh=mesh, in_specs=in_specs, out_specs=out_specs, check_vma=False)
```

```python
import functools

import jax
import jax.numpy as jnp
from jax import lax
from jax.experimental import pallas as pl
from jax.experimental.pallas import tpu as pltpu
from jax.sharding import PartitionSpec as P

F32 = jnp.float32
BF16 = jnp.bfloat16
VMEM = pl.BlockSpec(memory_space=pltpu.VMEM)
SMEM = pl.BlockSpec(memory_space=pltpu.SMEM)
TILE = 128


def call(kernel, outs, args, specs=None, scratch=(), after=(), alias={}, us=0):
    held = sum(a.size * a.dtype.itemsize for a in (*args, *outs))

    def body(*refs):
        kernel(*refs[: len(args)], *refs[len(args) + len(after) :])

    return pl.pallas_call(
        body,
        out_shape=outs,
        in_specs=(specs or [VMEM] * len(args)) + [pl.BlockSpec(memory_space=pl.ANY)] * len(after),
        input_output_aliases=alias,
        out_specs=[VMEM] * len(outs),
        scratch_shapes=scratch,
        compiler_params=pltpu.CompilerParams(vmem_limit_bytes=12 * 2**20 + 3 * held),
        cost_estimate=pl.CostEstimate(flops=int(us * 1.15e9), bytes_accessed=0, transcendentals=0),
    )(*args, *after)


def like(*shape, dtype=BF16):
    return jax.ShapeDtypeStruct(shape, dtype)


def swap(value, axis, size, mask):
    return lax.ppermute(value, axis, [(i, i ^ mask) for i in range(size)])


def tree(terms):
    while len(terms) > 1:
        terms = [sum(terms[i + 1 : i + 2], terms[i]) for i in range(0, len(terms), 2)]
    return terms[0]


def densify(n_z, values, rows, cols, count, dense, dense_t, other_t):
    me_row, me_col = lax.axis_index("row"), lax.axis_index("col")
    dense[...] = jnp.zeros_like(dense)
    dense_t[...] = jnp.zeros_like(dense_t)
    other_t[...] = jnp.zeros_like(other_t)

    def place(s, carry):
        far = rows[0, 0, s] ^ me_col
        inside = pl.multiple_of((far >> 1) * TILE, TILE)
        at = pl.multiple_of((far & 1) * n_z * TILE + inside, TILE)
        to = pl.multiple_of((cols[0, 0, s] ^ me_row) * TILE, TILE)
        tile = values[0, 0, s]
        dense[pl.ds(at, TILE), pl.ds(to, TILE)] = tile

        @pl.when((far & 1) == 0)
        def _():
            dense_t[pl.ds(to, TILE), pl.ds(inside, TILE)] = tile.T

        @pl.when((far & 1) == 1)
        def _():
            other_t[pl.ds(to, TILE), pl.ds(inside, TILE)] = tile.T

        return carry

    lax.fori_loop(0, count[0, 0], place, 0)


def forward(first, dense, *refs):
    *feats, out = refs
    size = out.shape[0]
    panel = jnp.concatenate([f[...] for f in feats], axis=0)
    out[...] = jnp.dot(
        dense[first : first + size, :], panel, preferred_element_type=F32
    ).astype(out.dtype)


def add_split(mine, other, *outs):
    rows = outs[0].shape[0]
    for k, out in enumerate(outs):
        part = pl.ds(k * rows, rows)
        out[...] = (mine[part, :].astype(F32) + other[part, :].astype(F32)).astype(out.dtype)


def relay(value, out):
    pass


def add_all(*refs):
    *terms, out = refs
    out[...] = tree([t[...].astype(F32) for t in terms]).astype(out.dtype)


def dense_layer(weight, cotangent, *refs):
    *terms, layer_out, summed, hidden_grad, grad_rows = refs
    total = tree([t[...].astype(F32) for t in terms]).astype(BF16)
    summed[...] = total
    hidden = jnp.dot(total, weight[...], preferred_element_type=F32)
    gate = jax.nn.sigmoid(hidden)
    layer_out[...] = (hidden * gate).astype(BF16)
    grad = (cotangent[0].astype(F32) * gate * (1.0 + hidden * (1.0 - gate))).astype(BF16)
    hidden_grad[...] = grad
    grad_rows[...] = lax.dot_general(
        grad, weight[...], (((1,), (1,)), ((), ())), preferred_element_type=F32
    ).astype(BF16)


def weight_term(n_row, scale, summed, hidden_grad, mine, other, whole):
    whole[...] = (
        lax.dot_general(
            summed[...], hidden_grad[...], (((0,), (0,)), ((), ())), preferred_element_type=F32
        )
        * scale
    )
    me_row, core = lax.axis_index("row"), lax.axis_index("col") & 1
    half = mine.shape[0]
    piece = half // n_row
    for k in range(n_row):
        inside = (me_row ^ k) * piece
        part = pl.ds(k * piece, piece)
        at = pl.multiple_of(core * half + inside, piece)
        mine[part, :] = whole[pl.ds(at, piece), :]
        at = pl.multiple_of((1 - core) * half + inside, piece)
        other[part, :] = whole[pl.ds(at, piece), :].astype(BF16)


def backward(dense_t, *refs):
    *grads, out = refs
    panel = jnp.concatenate([g[...] for g in grads], axis=0)
    out[...] = jnp.dot(dense_t[...], panel, preferred_element_type=F32).astype(out.dtype)


def messages(mine, other, final_w, own, *outs):
    own[...] = mine[:TILE, :] + other[:TILE, :].astype(F32)
    for k, out in enumerate(outs):
        part = pl.ds((k + 1) * TILE, TILE)
        out[:TILE, :] = (mine[part, :] + other[part, :].astype(F32)).astype(BF16)
        out[TILE:, :] = final_w[...]


def add_rows(own, *refs):
    *terms, out = refs
    total = own[...]
    for t in terms:
        total += t[:TILE, :].astype(F32)
    out[...] = total.astype(BF16)


def join(own, *refs):
    *others, out = refs
    me_row = lax.axis_index("row")
    piece = own.shape[0]
    out[pl.ds(pl.multiple_of(me_row * piece, piece), piece), :] = own[...]
    for k, ref in enumerate(others):
        at = pl.multiple_of((me_row ^ (k + 1)) * piece, piece)
        out[pl.ds(at, piece), :] = ref[TILE:, :]


def spread(mine, other, out):
    core = lax.axis_index("col") & 1
    half = mine.shape[0]
    out[pl.ds(pl.multiple_of(core * half, half), half), :] = mine[...].astype(F32)
    out[pl.ds(pl.multiple_of((1 - core) * half, half), half), :] = other[...].astype(F32)


def local(feats, weight, cotangent, tile_values, tile_rows, tile_cols, tile_count):
    width = feats.shape[2]
    n_row, n_col = lax.axis_size("row"), lax.axis_size("col")
    n_z = n_col // 2
    row_nodes, col_nodes = n_col * TILE, n_row * TILE
    half = row_nodes // 2
    row_swap = lambda x, k: swap(x, "row", n_row, k)
    z_swap = lambda x, k: swap(x, "col", n_col, 2 * k)
    core_swap = lambda x: swap(x, "col", n_col, 1)

    own = feats[0]
    panel = [own] + [row_swap(own, k) for k in range(1, n_row)]
    dense, dense_t, other_t = call(
        functools.partial(densify, n_z),
        [like(row_nodes, col_nodes), like(col_nodes, half), like(col_nodes, half)],
        (tile_values, tile_rows, tile_cols, tile_count),
        specs=[VMEM, SMEM, SMEM, SMEM],
    )
    other_t = core_swap(other_t)
    (other,) = call(functools.partial(forward, half), [like(half, width)], (dense, *panel))
    other = core_swap(other)
    (mine,) = call(
        functools.partial(forward, 0), [like(half, width, dtype=F32)], (dense, *panel)
    )
    parts = list(
        call(
            add_split,
            [like(TILE, width, dtype=F32)] + [like(TILE, width)] * (n_z - 1),
            (mine, other),
        )
    )
    bit, extra = 1, []
    while bit < n_z:
        far = [k for k in range(n_z) if k & bit and k % bit == 0]
        for k in sorted(far, reverse=True):
            got = z_swap(parts[k], bit)
            if k == bit:
                extra.append(got)
            else:
                (parts[k ^ bit],) = call(add_all, [like(TILE, width)], (parts[k ^ bit], got))
        bit *= 2
    terms = [parts[0]] + extra
    layer_out, summed, hidden_grad, grad_rows = call(
        dense_layer,
        [like(TILE, width)] * 4,
        (weight, cotangent, *terms),
        after=(other_t,),
    )
    piece = width // 2 // n_row
    mine_w, other_w = call(
        functools.partial(weight_term, n_row, (n_row * n_col * TILE) ** -0.5),
        [like(width // 2, width, dtype=F32), like(width // 2, width)],
        (summed, hidden_grad),
        scratch=[pltpu.VMEM((width, width), F32)],
    )
    other_w = core_swap(other_w)
    parts_w = call(add_split, [like(piece, width)] * n_row, (mine_w, other_w))
    terms_w = [parts_w[0]] + [row_swap(parts_w[k], k) for k in range(1, n_row)]
    same = [grad_rows] + [None] * (n_z - 1)
    bit = n_z // 2
    while bit:
        for k in range(0, n_z, 2 * bit):
            same[k | bit] = z_swap(same[k], bit)
            if bit > 1:
                (same[k | bit],) = call(
                    relay,
                    [like(TILE, width)],
                    (same[k | bit],),
                    after=terms_w[1 : n_row - 1],
                    alias={0: 0},
                )
        bit //= 2
    (plane_w,) = call(add_all, [like(piece, width)], terms_w)
    terms_w = [plane_w] + [z_swap(plane_w, k) for k in range(1, n_z)]
    (final_w,) = call(add_all, [like(piece, width)], terms_w, us=5)
    (other,) = call(backward, [like(col_nodes, width)], (other_t, *same))
    other = core_swap(other)
    (mine,) = call(backward, [like(col_nodes, width, dtype=F32)], (dense_t, *same))
    back, *parts = call(
        messages,
        [like(TILE, width, dtype=F32)] + [like(TILE + piece, width)] * (n_row - 1),
        (mine, other, final_w),
    )
    terms = [row_swap(part, k + 1) for k, part in enumerate(parts)]
    (half_w,) = call(join, [like(width // 2, width)], (final_w, *terms))
    other_w = core_swap(half_w)
    (feat_grad,) = call(add_rows, [like(TILE, width)], (back, *terms), after=(half_w,))
    (weight_grad,) = call(spread, [like(width, width, dtype=F32)], (half_w, other_w))
    return layer_out[None], feat_grad[None], weight_grad


def solution(mesh):
    in_specs = (
        P("col", "row", None),
        P(),
        P("row", "col", None),
        P("row", "col", None, None, None),
        P("row", "col", None),
        P("row", "col", None),
        P("row", "col"),
    )
    out_specs = (P("row", "col", None), P("col", "row", None), P())
    return jax.shard_map(local, mesh=mesh, in_specs=in_specs, out_specs=out_specs, check_vma=False)
```

```python
import functools

import jax
import jax.numpy as jnp
from jax import lax
from jax.experimental import pallas as pl
from jax.experimental.pallas import tpu as pltpu
from jax.sharding import PartitionSpec as P

F32 = jnp.float32
BF16 = jnp.bfloat16
VMEM = pl.BlockSpec(memory_space=pltpu.VMEM)
SMEM = pl.BlockSpec(memory_space=pltpu.SMEM)
TILE = 128


def call(kernel, outs, args, specs=None, scratch=(), after=(), alias={}, us=0):
    held = sum(a.size * a.dtype.itemsize for a in (*args, *outs))

    def body(*refs):
        kernel(*refs[: len(args)], *refs[len(args) + len(after) :])

    return pl.pallas_call(
        body,
        out_shape=outs,
        in_specs=(specs or [VMEM] * len(args)) + [pl.BlockSpec(memory_space=pl.ANY)] * len(after),
        input_output_aliases=alias,
        out_specs=[VMEM] * len(outs),
        scratch_shapes=scratch,
        compiler_params=pltpu.CompilerParams(vmem_limit_bytes=12 * 2**20 + 3 * held),
        cost_estimate=pl.CostEstimate(flops=int(us * 1.15e9), bytes_accessed=0, transcendentals=0),
    )(*args, *after)


def like(*shape, dtype=BF16):
    return jax.ShapeDtypeStruct(shape, dtype)


def swap(value, axis, size, mask):
    return lax.ppermute(value, axis, [(i, i ^ mask) for i in range(size)])


def tree(terms):
    while len(terms) > 1:
        terms = [sum(terms[i + 1 : i + 2], terms[i]) for i in range(0, len(terms), 2)]
    return terms[0]


def densify(n_z, values, rows, cols, count, dense, dense_t, other_t):
    me_row, me_col = lax.axis_index("row"), lax.axis_index("col")
    dense[...] = jnp.zeros_like(dense)
    dense_t[...] = jnp.zeros_like(dense_t)
    other_t[...] = jnp.zeros_like(other_t)

    def place(s, carry):
        far = rows[0, 0, s] ^ me_col
        inside = pl.multiple_of((far >> 1) * TILE, TILE)
        chip = far >> 1
        part = (far & 1) * n_z + (1 - (chip & 1)) * (n_z // 2) + (chip >> 1)
        at = pl.multiple_of(part * TILE, TILE)
        to = pl.multiple_of((cols[0, 0, s] ^ me_row) * TILE, TILE)
        tile = values[0, 0, s]
        dense[pl.ds(at, TILE), pl.ds(to, TILE)] = tile

        @pl.when((far & 1) == 0)
        def _():
            dense_t[pl.ds(to, TILE), pl.ds(inside, TILE)] = tile.T

        @pl.when((far & 1) == 1)
        def _():
            other_t[pl.ds(to, TILE), pl.ds(inside, TILE)] = tile.T

        return carry

    lax.fori_loop(0, count[0, 0], place, 0)


def forward(first, dense, *refs):
    *feats, out = refs
    size = out.shape[0]
    panel = jnp.concatenate([f[...] for f in feats], axis=0)
    out[...] = jnp.dot(
        dense[first : first + size, :], panel, preferred_element_type=F32
    ).astype(out.dtype)


def add_split(mine, other, *outs):
    rows = outs[0].shape[0]
    for k, out in enumerate(outs):
        part = pl.ds(k * rows, rows)
        out[...] = (mine[part, :].astype(F32) + other[part, :].astype(F32)).astype(out.dtype)


def relay(value, out):
    pass


def add_all(*refs):
    *terms, out = refs
    out[...] = tree([t[...].astype(F32) for t in terms]).astype(out.dtype)


def dense_layer(weight, cotangent, *refs):
    *terms, hidden_out, summed, hidden_grad, grad_rows = refs
    total = tree([t[...].astype(F32) for t in terms]).astype(BF16)
    summed[...] = total
    hidden = jnp.dot(total, weight[...], preferred_element_type=F32)
    hidden_out[...] = hidden
    gate = jax.nn.sigmoid(hidden)
    grad = (cotangent[0].astype(F32) * gate * (1.0 + hidden * (1.0 - gate))).astype(BF16)
    hidden_grad[...] = grad
    grad_rows[...] = lax.dot_general(
        grad, weight[...], (((1,), (1,)), ((), ())), preferred_element_type=F32
    ).astype(BF16)


def activation(hidden, out, done):
    done[...] = jnp.zeros_like(done)
    out[...] = (hidden[...] * jax.nn.sigmoid(hidden[...])).astype(BF16)


def weight_term(n_row, scale, summed, hidden_grad, mine, other, whole):
    whole[...] = (
        lax.dot_general(
            summed[...], hidden_grad[...], (((0,), (0,)), ((), ())), preferred_element_type=F32
        )
        * scale
    )
    me_row, core = lax.axis_index("row"), lax.axis_index("col") & 1
    half = mine.shape[0]
    piece = half // n_row
    for k in range(n_row):
        inside = (me_row ^ k) * piece
        part = pl.ds(k * piece, piece)
        at = pl.multiple_of(core * half + inside, piece)
        mine[part, :] = whole[pl.ds(at, piece), :]
        at = pl.multiple_of((1 - core) * half + inside, piece)
        other[part, :] = whole[pl.ds(at, piece), :].astype(BF16)


def backward(dense_t, *refs):
    *grads, out = refs
    panel = jnp.concatenate([g[...] for g in grads], axis=0)
    out[...] = jnp.dot(dense_t[...], panel, preferred_element_type=F32).astype(out.dtype)


def messages(mine, other, final_w, own, *outs):
    own[...] = mine[:TILE, :] + other[:TILE, :].astype(F32)
    for k, out in enumerate(outs):
        part = pl.ds((k + 1) * TILE, TILE)
        out[:TILE, :] = (mine[part, :] + other[part, :].astype(F32)).astype(BF16)
        out[TILE:, :] = final_w[...]


def add_rows(own, *refs):
    *terms, out = refs
    total = own[...]
    for t in terms:
        total += t[:TILE, :].astype(F32)
    out[...] = total.astype(BF16)


def join(own, *refs):
    *others, out = refs
    me_row = lax.axis_index("row")
    piece = own.shape[0]
    out[pl.ds(pl.multiple_of(me_row * piece, piece), piece), :] = own[...]
    for k, ref in enumerate(others):
        at = pl.multiple_of((me_row ^ (k + 1)) * piece, piece)
        out[pl.ds(at, piece), :] = ref[TILE:, :]


def spread(mine, other, out):
    core = lax.axis_index("col") & 1
    half = mine.shape[0]
    out[pl.ds(pl.multiple_of(core * half, half), half), :] = mine[...].astype(F32)
    out[pl.ds(pl.multiple_of((1 - core) * half, half), half), :] = other[...].astype(F32)


def local(feats, weight, cotangent, tile_values, tile_rows, tile_cols, tile_count):
    width = feats.shape[2]
    n_row, n_col = lax.axis_size("row"), lax.axis_size("col")
    n_z = n_col // 2
    row_nodes, col_nodes = n_col * TILE, n_row * TILE
    half = row_nodes // 2
    row_swap = lambda x, k: swap(x, "row", n_row, k)
    z_swap = lambda x, k: swap(x, "col", n_col, 2 * k)
    core_swap = lambda x: swap(x, "col", n_col, 1)

    own = feats[0]
    panel = [own] + [row_swap(own, k) for k in range(1, n_row)]
    dense, dense_t, other_t = call(
        functools.partial(densify, n_z),
        [like(row_nodes, col_nodes), like(col_nodes, half), like(col_nodes, half)],
        (tile_values, tile_rows, tile_cols, tile_count),
        specs=[VMEM, SMEM, SMEM, SMEM],
    )
    other_t = core_swap(other_t)
    quarter, parts = half // 2, [None] * n_z
    for odd in (1, 0):
        first = (1 - odd) * quarter
        (other,) = call(
            functools.partial(forward, half + first),
            [like(quarter, width)],
            (dense, *panel),
        )
        other = core_swap(other)
        (mine,) = call(
            functools.partial(forward, first), [like(quarter, width, dtype=F32)], (dense, *panel)
        )
        outs = [like(TILE, width, dtype=BF16 if k else F32) for k in range(odd, n_z, 2)]
        parts[odd::2] = call(add_split, outs, (mine, other))
    bit, extra = 1, []
    while bit < n_z:
        far = [k for k in range(n_z) if k & bit and k % bit == 0]
        for k in sorted(far, reverse=True):
            got = z_swap(parts[k], bit)
            if k == bit:
                extra.append(got)
            else:
                (parts[k ^ bit],) = call(add_all, [like(TILE, width)], (parts[k ^ bit], got))
        bit *= 2
    terms = [parts[0]] + extra
    hidden, summed, hidden_grad, grad_rows = call(
        dense_layer,
        [like(TILE, width, dtype=F32)] + [like(TILE, width)] * 3,
        (weight, cotangent, *terms),
    )
    piece = width // 2 // n_row
    mine_w, other_w = call(
        functools.partial(weight_term, n_row, (n_row * n_col * TILE) ** -0.5),
        [like(width // 2, width, dtype=F32), like(width // 2, width)],
        (summed, hidden_grad),
        scratch=[pltpu.VMEM((width, width), F32)],
    )
    other_w = core_swap(other_w)
    parts_w = call(add_split, [like(piece, width)] * n_row, (mine_w, other_w), after=(other_t,))
    terms_w = [parts_w[0]] + [row_swap(parts_w[k], k) for k in range(1, n_row)]
    same = [grad_rows] + [None] * (n_z - 1)
    bit = n_z // 2
    while bit:
        for k in range(0, n_z, 2 * bit):
            same[k | bit] = z_swap(same[k], bit)
            if bit > 1:
                (same[k | bit],) = call(
                    relay,
                    [like(TILE, width)],
                    (same[k | bit],),
                    after=terms_w[1 : n_row - 1],
                    alias={0: 0},
                )
        bit //= 2
    (plane_w,) = call(add_all, [like(piece, width)], terms_w)
    terms_w = [plane_w] + [z_swap(plane_w, k) for k in range(1, n_z)]
    (final_w,) = call(add_all, [like(piece, width)], terms_w, us=5)
    (other,) = call(backward, [like(col_nodes, width)], (other_t, *same))
    other = core_swap(other)
    (mine,) = call(backward, [like(col_nodes, width, dtype=F32)], (dense_t, *same))
    back, *parts = call(
        messages,
        [like(TILE, width, dtype=F32)] + [like(TILE + piece, width)] * (n_row - 1),
        (mine, other, final_w),
    )
    terms = [row_swap(part, k + 1) for k, part in enumerate(parts)]
    layer_out, done = call(
        activation, [like(TILE, width), like(8, TILE, dtype=F32)], (hidden,), us=1
    )
    (half_w,) = call(join, [like(width // 2, width)], (final_w, *terms), after=(done,))
    other_w = core_swap(half_w)
    (feat_grad,) = call(add_rows, [like(TILE, width)], (back, *terms), after=(half_w,))
    (weight_grad,) = call(spread, [like(width, width, dtype=F32)], (half_w, other_w))
    return layer_out[None], feat_grad[None], weight_grad


def solution(mesh):
    in_specs = (
        P("col", "row", None),
        P(),
        P("row", "col", None),
        P("row", "col", None, None, None),
        P("row", "col", None),
        P("row", "col", None),
        P("row", "col"),
    )
    out_specs = (P("row", "col", None), P("col", "row", None), P())
    return jax.shard_map(local, mesh=mesh, in_specs=in_specs, out_specs=out_specs, check_vma=False)
```

```python
import functools

import jax
import jax.numpy as jnp
from jax import lax
from jax.experimental import pallas as pl
from jax.experimental.pallas import tpu as pltpu
from jax.sharding import PartitionSpec as P

F32 = jnp.float32
BF16 = jnp.bfloat16
VMEM = pl.BlockSpec(memory_space=pltpu.VMEM)
SMEM = pl.BlockSpec(memory_space=pltpu.SMEM)
TILE = 128


def call(kernel, outs, args, specs=None, scratch=(), after=(), us=0):
    held = sum(a.size * a.dtype.itemsize for a in (*args, *outs))

    def body(*refs):
        kernel(*refs[: len(args)], *refs[len(args) + len(after) :])

    return pl.pallas_call(
        body,
        out_shape=outs,
        in_specs=(specs or [VMEM] * len(args)) + [pl.BlockSpec(memory_space=pl.ANY)] * len(after),
        out_specs=[VMEM] * len(outs),
        scratch_shapes=scratch,
        compiler_params=pltpu.CompilerParams(vmem_limit_bytes=12 * 2**20 + 3 * held),
        cost_estimate=pl.CostEstimate(flops=int(us * 1.15e9), bytes_accessed=0, transcendentals=0),
    )(*args, *after)


def like(*shape, dtype=BF16):
    return jax.ShapeDtypeStruct(shape, dtype)


def swap(value, axis, size, mask):
    return lax.ppermute(value, axis, [(i, i ^ mask) for i in range(size)])


def tree(terms):
    while len(terms) > 1:
        terms = [sum(terms[i + 1 : i + 2], terms[i]) for i in range(0, len(terms), 2)]
    return terms[0]


def densify(n_z, values, rows, cols, count, dense, dense_t, other_t):
    me_row, me_col = lax.axis_index("row"), lax.axis_index("col")
    dense[...] = jnp.zeros_like(dense)
    dense_t[...] = jnp.zeros_like(dense_t)
    other_t[...] = jnp.zeros_like(other_t)

    def place(s, carry):
        far = rows[0, 0, s] ^ me_col
        inside = pl.multiple_of((far >> 1) * TILE, TILE)
        chip = far >> 1
        part = (far & 1) * n_z + (1 - (chip & 1)) * (n_z // 2) + (chip >> 1)
        at = pl.multiple_of(part * TILE, TILE)
        to = pl.multiple_of((cols[0, 0, s] ^ me_row) * TILE, TILE)
        tile = values[0, 0, s]
        dense[pl.ds(at, TILE), pl.ds(to, TILE)] = tile

        @pl.when((far & 1) == 0)
        def _():
            dense_t[pl.ds(to, TILE), pl.ds(inside, TILE)] = tile.T

        @pl.when((far & 1) == 1)
        def _():
            other_t[pl.ds(to, TILE), pl.ds(inside, TILE)] = tile.T

        return carry

    lax.fori_loop(0, count[0, 0], place, 0)


def forward(first, dense, *refs):
    *feats, out = refs
    size = out.shape[0]
    panel = jnp.concatenate([f[...] for f in feats], axis=0)
    out[...] = jnp.dot(
        dense[first : first + size, :], panel, preferred_element_type=F32
    ).astype(out.dtype)


def add_split(mine, other, *outs):
    rows = outs[0].shape[0]
    for k, out in enumerate(outs):
        part = pl.ds(k * rows, rows)
        out[...] = (mine[part, :].astype(F32) + other[part, :].astype(F32)).astype(out.dtype)


def relay(value, out):
    out[...] = value[...]


def add_all(*refs):
    *terms, out = refs
    out[...] = tree([t[...].astype(F32) for t in terms]).astype(out.dtype)


def dense_layer(weight, cotangent, *refs):
    *terms, hidden_out, summed, hidden_grad, grad_rows = refs
    total = tree([t[...].astype(F32) for t in terms]).astype(BF16)
    summed[...] = total
    hidden = jnp.dot(total, weight[...], preferred_element_type=F32)
    hidden_out[...] = hidden
    gate = jax.nn.sigmoid(hidden)
    grad = (cotangent[0].astype(F32) * gate * (1.0 + hidden * (1.0 - gate))).astype(BF16)
    hidden_grad[...] = grad
    grad_rows[...] = lax.dot_general(
        grad, weight[...], (((1,), (1,)), ((), ())), preferred_element_type=F32
    ).astype(BF16)


def activation(hidden, out, done):
    done[...] = jnp.zeros_like(done)
    out[...] = (hidden[...] * jax.nn.sigmoid(hidden[...])).astype(BF16)


def weight_term(n_row, scale, summed, hidden_grad, mine, other, whole):
    whole[...] = (
        lax.dot_general(
            summed[...], hidden_grad[...], (((0,), (0,)), ((), ())), preferred_element_type=F32
        )
        * scale
    )
    me_row, core = lax.axis_index("row"), lax.axis_index("col") & 1
    half = mine.shape[0]
    piece = half // n_row
    for k in range(n_row):
        inside = (me_row ^ k) * piece
        part = pl.ds(k * piece, piece)
        at = pl.multiple_of(core * half + inside, piece)
        mine[part, :] = whole[pl.ds(at, piece), :]
        at = pl.multiple_of((1 - core) * half + inside, piece)
        other[part, :] = whole[pl.ds(at, piece), :].astype(BF16)


def backward(dense_t, *refs):
    *grads, out = refs
    panel = jnp.concatenate([g[...] for g in grads], axis=0)
    out[...] = jnp.dot(dense_t[...], panel, preferred_element_type=F32).astype(out.dtype)


def messages(mine, other, final_w, own, *outs):
    own[...] = mine[:TILE, :] + other[:TILE, :].astype(F32)
    for k, out in enumerate(outs):
        part = pl.ds((k + 1) * TILE, TILE)
        out[:TILE, :] = (mine[part, :] + other[part, :].astype(F32)).astype(BF16)
        out[TILE:, :] = final_w[...]


def add_rows(own, *refs):
    *terms, out = refs
    total = own[...]
    for t in terms:
        total += t[:TILE, :].astype(F32)
    out[...] = total.astype(BF16)


def join(own, *refs):
    *others, out = refs
    me_row = lax.axis_index("row")
    piece = own.shape[0]
    out[pl.ds(pl.multiple_of(me_row * piece, piece), piece), :] = own[...]
    for k, ref in enumerate(others):
        at = pl.multiple_of((me_row ^ (k + 1)) * piece, piece)
        out[pl.ds(at, piece), :] = ref[TILE:, :]


def spread(mine, other, out):
    core = lax.axis_index("col") & 1
    half = mine.shape[0]
    out[pl.ds(pl.multiple_of(core * half, half), half), :] = mine[...].astype(F32)
    out[pl.ds(pl.multiple_of((1 - core) * half, half), half), :] = other[...].astype(F32)


def local(feats, weight, cotangent, tile_values, tile_rows, tile_cols, tile_count):
    width = feats.shape[2]
    n_row, n_col = lax.axis_size("row"), lax.axis_size("col")
    n_z = n_col // 2
    row_nodes, col_nodes = n_col * TILE, n_row * TILE
    half = row_nodes // 2
    row_swap = lambda x, k: swap(x, "row", n_row, k)
    z_swap = lambda x, k: swap(x, "col", n_col, 2 * k)
    core_swap = lambda x: swap(x, "col", n_col, 1)

    own = feats[0]
    panel = [own] + [row_swap(own, k) for k in range(1, n_row)]
    dense, dense_t, other_t = call(
        functools.partial(densify, n_z),
        [like(row_nodes, col_nodes), like(col_nodes, half), like(col_nodes, half)],
        (tile_values, tile_rows, tile_cols, tile_count),
        specs=[VMEM, SMEM, SMEM, SMEM],
    )
    other_t = core_swap(other_t)
    quarter, parts = half // 2, [None] * n_z
    for odd in (1, 0):
        first = (1 - odd) * quarter
        (other,) = call(
            functools.partial(forward, half + first),
            [like(quarter, width)],
            (dense, *panel),
        )
        other = core_swap(other)
        (mine,) = call(
            functools.partial(forward, first), [like(quarter, width, dtype=F32)], (dense, *panel)
        )
        outs = [like(TILE, width, dtype=BF16 if k else F32) for k in range(odd, n_z, 2)]
        parts[odd::2] = call(add_split, outs, (mine, other))
    bit, extra = 1, []
    while bit < n_z:
        far = [k for k in range(n_z) if k & bit and k % bit == 0]
        for k in sorted(far, reverse=True):
            got = z_swap(parts[k], bit)
            if k == bit:
                extra.append(got)
            else:
                (parts[k ^ bit],) = call(add_all, [like(TILE, width)], (parts[k ^ bit], got))
        bit *= 2
    terms = [parts[0]] + extra
    hidden, summed, hidden_grad, grad_rows = call(
        dense_layer,
        [like(TILE, width, dtype=F32)] + [like(TILE, width)] * 3,
        (weight, cotangent, *terms),
    )
    piece = width // 2 // n_row
    mine_w, other_w = call(
        functools.partial(weight_term, n_row, (n_row * n_col * TILE) ** -0.5),
        [like(width // 2, width, dtype=F32), like(width // 2, width)],
        (summed, hidden_grad),
        scratch=[pltpu.VMEM((width, width), F32)],
    )
    other_w = core_swap(other_w)
    parts_w = call(add_split, [like(piece, width)] * n_row, (mine_w, other_w), after=(other_t,))
    terms_w = {k: row_swap(parts_w[k], k) for k in reversed(range(1, n_row))}
    terms_w[0] = parts_w[0]
    terms_w = [terms_w[k] for k in range(n_row)]
    same = [grad_rows] + [None] * (n_z - 1)
    bit = n_z // 2
    while bit:
        for k in range(0, n_z, 2 * bit):
            same[k | bit] = z_swap(same[k], bit)
            if bit > 1:
                (same[k | bit],) = call(
                    relay, [like(TILE, width)], (same[k | bit],), after=tuple(terms_w[2:])
                )
        bit //= 2
    (plane_w,) = call(add_all, [like(piece, width)], terms_w)
    terms_w = [plane_w] + [z_swap(plane_w, k) for k in range(1, n_z)]
    (final_w,) = call(add_all, [like(piece, width)], terms_w, us=5)
    (other,) = call(backward, [like(col_nodes, width)], (other_t, *same))
    other = core_swap(other)
    (mine,) = call(backward, [like(col_nodes, width, dtype=F32)], (dense_t, *same))
    back, *parts = call(
        messages,
        [like(TILE, width, dtype=F32)] + [like(TILE + piece, width)] * (n_row - 1),
        (mine, other, final_w),
    )
    terms = [row_swap(parts[k - 1], k) for k in reversed(range(1, n_row))][::-1]
    layer_out, done = call(
        activation, [like(TILE, width), like(8, TILE, dtype=F32)], (hidden,), us=1
    )
    (half_w,) = call(join, [like(width // 2, width)], (final_w, *terms), after=(done,))
    other_w = core_swap(half_w)
    (feat_grad,) = call(add_rows, [like(TILE, width)], (back, *terms), after=(half_w,))
    (weight_grad,) = call(spread, [like(width, width, dtype=F32)], (half_w, other_w))
    return layer_out[None], feat_grad[None], weight_grad


def solution(mesh):
    in_specs = (
        P("col", "row", None),
        P(),
        P("row", "col", None),
        P("row", "col", None, None, None),
        P("row", "col", None),
        P("row", "col", None),
        P("row", "col"),
    )
    out_specs = (P("row", "col", None), P("col", "row", None), P())
    return jax.shard_map(local, mesh=mesh, in_specs=in_specs, out_specs=out_specs, check_vma=False)
```

```python
import functools

import jax
import jax.numpy as jnp
from jax import lax
from jax.experimental import pallas as pl
from jax.experimental.pallas import tpu as pltpu
from jax.sharding import PartitionSpec as P

F32 = jnp.float32
BF16 = jnp.bfloat16
VMEM = pl.BlockSpec(memory_space=pltpu.VMEM)
SMEM = pl.BlockSpec(memory_space=pltpu.SMEM)
TILE = 128


def call(kernel, outs, args, specs=None, scratch=(), after=(), us=0):
    held = sum(a.size * a.dtype.itemsize for a in (*args, *outs))

    def body(*refs):
        kernel(*refs[: len(args)], *refs[len(args) + len(after) :])

    return pl.pallas_call(
        body,
        out_shape=outs,
        in_specs=(specs or [VMEM] * len(args)) + [pl.BlockSpec(memory_space=pl.ANY)] * len(after),
        out_specs=[VMEM] * len(outs),
        scratch_shapes=scratch,
        compiler_params=pltpu.CompilerParams(vmem_limit_bytes=12 * 2**20 + 3 * held),
        cost_estimate=pl.CostEstimate(flops=int(us * 1.15e9), bytes_accessed=0, transcendentals=0),
    )(*args, *after)


def like(*shape, dtype=BF16):
    return jax.ShapeDtypeStruct(shape, dtype)


def swap(value, axis, size, mask):
    return lax.ppermute(value, axis, [(i, i ^ mask) for i in range(size)])


def tree(terms):
    while len(terms) > 1:
        terms = [sum(terms[i + 1 : i + 2], terms[i]) for i in range(0, len(terms), 2)]
    return terms[0]


def densify(n_z, values, rows, cols, count, dense, dense_t, other_t):
    me_row, me_col = lax.axis_index("row"), lax.axis_index("col")
    dense[...] = jnp.zeros_like(dense)
    dense_t[...] = jnp.zeros_like(dense_t)
    other_t[...] = jnp.zeros_like(other_t)

    def place(s, carry):
        far = rows[0, 0, s] ^ me_col
        inside = pl.multiple_of((far >> 1) * TILE, TILE)
        chip = far >> 1
        part = (far & 1) * n_z + (1 - (chip & 1)) * (n_z // 2) + (chip >> 1)
        at = pl.multiple_of(part * TILE, TILE)
        to = pl.multiple_of((cols[0, 0, s] ^ me_row) * TILE, TILE)
        tile = values[0, 0, s]
        dense[pl.ds(at, TILE), pl.ds(to, TILE)] = tile

        @pl.when((far & 1) == 0)
        def _():
            dense_t[pl.ds(to, TILE), pl.ds(inside, TILE)] = tile.T

        @pl.when((far & 1) == 1)
        def _():
            other_t[pl.ds(to, TILE), pl.ds(inside, TILE)] = tile.T

        return carry

    lax.fori_loop(0, count[0, 0], place, 0)


def forward(first, dense, *refs):
    *feats, out = refs
    size = out.shape[0]
    panel = jnp.concatenate([f[...] for f in feats], axis=0)
    out[...] = jnp.dot(
        dense[first : first + size, :], panel, preferred_element_type=F32
    ).astype(out.dtype)


def add_split(mine, other, *outs):
    rows = outs[0].shape[0]
    for k, out in enumerate(outs):
        part = pl.ds(k * rows, rows)
        out[...] = (mine[part, :].astype(F32) + other[part, :].astype(F32)).astype(out.dtype)


def relay(value, out):
    out[...] = value[...]


def add_all(*refs):
    *terms, out = refs
    out[...] = tree([t[...].astype(F32) for t in terms]).astype(out.dtype)


def dense_layer(weight, cotangent, *refs):
    *terms, hidden_out, summed, hidden_grad, grad_rows = refs
    total = tree([t[...].astype(F32) for t in terms]).astype(BF16)
    summed[...] = total
    hidden = jnp.dot(total, weight[...], preferred_element_type=F32)
    hidden_out[...] = hidden
    gate = jax.nn.sigmoid(hidden)
    grad = (cotangent[0].astype(F32) * gate * (1.0 + hidden * (1.0 - gate))).astype(BF16)
    hidden_grad[...] = grad
    grad_rows[...] = lax.dot_general(
        grad, weight[...], (((1,), (1,)), ((), ())), preferred_element_type=F32
    ).astype(BF16)


def activation(hidden, out, done):
    done[...] = jnp.zeros_like(done)
    out[...] = (hidden[...] * jax.nn.sigmoid(hidden[...])).astype(BF16)


def weight_term(n_row, scale, summed, hidden_grad, mine, other, whole):
    whole[...] = (
        lax.dot_general(
            summed[...], hidden_grad[...], (((0,), (0,)), ((), ())), preferred_element_type=F32
        )
        * scale
    )
    me_row, core = lax.axis_index("row"), lax.axis_index("col") & 1
    half = mine.shape[0]
    piece = half // n_row
    for k in range(n_row):
        inside = (me_row ^ k) * piece
        part = pl.ds(k * piece, piece)
        at = pl.multiple_of(core * half + inside, piece)
        mine[part, :] = whole[pl.ds(at, piece), :]
        at = pl.multiple_of((1 - core) * half + inside, piece)
        other[part, :] = whole[pl.ds(at, piece), :].astype(BF16)


def backward(dense_t, *refs):
    *grads, out = refs
    panel = jnp.concatenate([g[...] for g in grads], axis=0)
    out[...] = jnp.dot(dense_t[...], panel, preferred_element_type=F32).astype(out.dtype)


def messages(mine, other, final_w, own, *outs):
    own[...] = mine[:TILE, :] + other[:TILE, :].astype(F32)
    for k, out in enumerate(outs):
        part = pl.ds((k + 1) * TILE, TILE)
        out[:TILE, :] = (mine[part, :] + other[part, :].astype(F32)).astype(BF16)
        out[TILE:, :] = final_w[...]


def add_rows(own, *refs):
    *terms, out = refs
    total = own[...]
    for t in terms:
        total += t[:TILE, :].astype(F32)
    out[...] = total.astype(BF16)


def join(own, *refs):
    *others, out = refs
    me_row = lax.axis_index("row")
    piece = own.shape[0]
    out[pl.ds(pl.multiple_of(me_row * piece, piece), piece), :] = own[...]
    for k, ref in enumerate(others):
        at = pl.multiple_of((me_row ^ (k + 1)) * piece, piece)
        out[pl.ds(at, piece), :] = ref[TILE:, :]


def spread(mine, other, out):
    core = lax.axis_index("col") & 1
    half = mine.shape[0]
    out[pl.ds(pl.multiple_of(core * half, half), half), :] = mine[...].astype(F32)
    out[pl.ds(pl.multiple_of((1 - core) * half, half), half), :] = other[...].astype(F32)


def local(feats, weight, cotangent, tile_values, tile_rows, tile_cols, tile_count):
    width = feats.shape[2]
    n_row, n_col = lax.axis_size("row"), lax.axis_size("col")
    n_z = n_col // 2
    row_nodes, col_nodes = n_col * TILE, n_row * TILE
    half = row_nodes // 2
    row_swap = lambda x, k: swap(x, "row", n_row, k)
    z_swap = lambda x, k: swap(x, "col", n_col, 2 * k)
    core_swap = lambda x: swap(x, "col", n_col, 1)

    own = feats[0]
    panel = [own] + [row_swap(own, k) for k in range(1, n_row)]
    dense, dense_t, other_t = call(
        functools.partial(densify, n_z),
        [like(row_nodes, col_nodes), like(col_nodes, half), like(col_nodes, half)],
        (tile_values, tile_rows, tile_cols, tile_count),
        specs=[VMEM, SMEM, SMEM, SMEM],
    )
    other_t = core_swap(other_t)
    quarter, parts = half // 2, [None] * n_z
    for odd in (1, 0):
        first = (1 - odd) * quarter
        (other,) = call(
            functools.partial(forward, half + first),
            [like(quarter, width)],
            (dense, *panel),
        )
        other = core_swap(other)
        (mine,) = call(
            functools.partial(forward, first), [like(quarter, width, dtype=F32)], (dense, *panel)
        )
        outs = [like(TILE, width, dtype=BF16 if k else F32) for k in range(odd, n_z, 2)]
        parts[odd::2] = call(add_split, outs, (mine, other))
    bit, extra = 1, []
    while bit < n_z:
        far = [k for k in range(n_z) if k & bit and k % bit == 0]
        for k in sorted(far, reverse=True):
            got = z_swap(parts[k], bit)
            if k == bit:
                extra.append(got)
            else:
                (parts[k ^ bit],) = call(add_all, [like(TILE, width)], (parts[k ^ bit], got))
        bit *= 2
    terms = [parts[0]] + extra
    hidden, summed, hidden_grad, grad_rows = call(
        dense_layer,
        [like(TILE, width, dtype=F32)] + [like(TILE, width)] * 3,
        (weight, cotangent, *terms),
    )
    piece = width // 2 // n_row
    mine_w, other_w = call(
        functools.partial(weight_term, n_row, (n_row * n_col * TILE) ** -0.5),
        [like(width // 2, width, dtype=F32), like(width // 2, width)],
        (summed, hidden_grad),
        scratch=[pltpu.VMEM((width, width), F32)],
    )
    other_w = core_swap(other_w)
    parts_w = call(add_split, [like(piece, width)] * n_row, (mine_w, other_w), after=(other_t,))
    terms_w = [parts_w[0]] + [row_swap(parts_w[k], k) for k in range(1, n_row)]
    same = [grad_rows] + [None] * (n_z - 1)
    bit = n_z // 2
    while bit:
        for k in range(0, n_z, 2 * bit):
            same[k | bit] = z_swap(same[k], bit)
            if bit > 1:
                (same[k | bit],) = call(
                    relay, [like(TILE, width)], (same[k | bit],), after=terms_w[1 : n_row - 1]
                )
        bit //= 2
    (plane_w,) = call(add_all, [like(piece, width)], terms_w)
    terms_w = [plane_w] + [z_swap(plane_w, k) for k in range(1, n_z)]
    (final_w,) = call(add_all, [like(piece, width)], terms_w, us=5)
    (other,) = call(backward, [like(col_nodes, width)], (other_t, *same))
    other = core_swap(other)
    (mine,) = call(backward, [like(col_nodes, width, dtype=F32)], (dense_t, *same))
    back, *parts = call(
        messages,
        [like(TILE, width, dtype=F32)] + [like(TILE + piece, width)] * (n_row - 1),
        (mine, other, final_w),
    )
    terms = [row_swap(part, k + 1) for k, part in enumerate(parts)]
    layer_out, done = call(
        activation, [like(TILE, width), like(8, TILE, dtype=F32)], (hidden,), us=1
    )
    (half_w,) = call(join, [like(width // 2, width)], (final_w, *terms), after=(done,))
    other_w = core_swap(half_w)
    (feat_grad,) = call(add_rows, [like(TILE, width)], (back, *terms), after=(half_w,))
    (weight_grad,) = call(spread, [like(width, width, dtype=F32)], (half_w, other_w))
    return layer_out[None], feat_grad[None], weight_grad


def solution(mesh):
    in_specs = (
        P("col", "row", None),
        P(),
        P("row", "col", None),
        P("row", "col", None, None, None),
        P("row", "col", None),
        P("row", "col", None),
        P("row", "col"),
    )
    out_specs = (P("row", "col", None), P("col", "row", None), P())
    return jax.shard_map(local, mesh=mesh, in_specs=in_specs, out_specs=out_specs, check_vma=False)
```

```python
import functools

import jax
import jax.numpy as jnp
from jax import lax
from jax.experimental import pallas as pl
from jax.experimental.pallas import tpu as pltpu
from jax.sharding import PartitionSpec as P

F32 = jnp.float32
BF16 = jnp.bfloat16
VMEM = pl.BlockSpec(memory_space=pltpu.VMEM)
SMEM = pl.BlockSpec(memory_space=pltpu.SMEM)
TILE = 128


def call(kernel, outs, args, specs=None, scratch=(), after=(), us=0):
    held = sum(a.size * a.dtype.itemsize for a in (*args, *outs))

    def body(*refs):
        kernel(*refs[: len(args)], *refs[len(args) + len(after) :])

    return pl.pallas_call(
        body,
        out_shape=outs,
        in_specs=(specs or [VMEM] * len(args)) + [pl.BlockSpec(memory_space=pl.ANY)] * len(after),
        out_specs=[VMEM] * len(outs),
        scratch_shapes=scratch,
        compiler_params=pltpu.CompilerParams(vmem_limit_bytes=12 * 2**20 + 3 * held),
        cost_estimate=pl.CostEstimate(flops=int(us * 1.15e9), bytes_accessed=0, transcendentals=0),
    )(*args, *after)


def like(*shape, dtype=BF16):
    return jax.ShapeDtypeStruct(shape, dtype)


def swap(value, axis, size, mask):
    return lax.ppermute(value, axis, [(i, i ^ mask) for i in range(size)])


def tree(terms):
    while len(terms) > 1:
        terms = [sum(terms[i + 1 : i + 2], terms[i]) for i in range(0, len(terms), 2)]
    return terms[0]


def densify(n_z, values, rows, cols, count, dense, dense_t, other_t):
    me_row, me_col = lax.axis_index("row"), lax.axis_index("col")
    dense[...] = jnp.zeros_like(dense)
    dense_t[...] = jnp.zeros_like(dense_t)
    other_t[...] = jnp.zeros_like(other_t)

    def place(s, carry):
        far = rows[0, 0, s] ^ me_col
        inside = pl.multiple_of((far >> 1) * TILE, TILE)
        chip = far >> 1
        part = (far & 1) * n_z + (1 - (chip & 1)) * (n_z // 2) + (chip >> 1)
        at = pl.multiple_of(part * TILE, TILE)
        to = pl.multiple_of((cols[0, 0, s] ^ me_row) * TILE, TILE)
        tile = values[0, 0, s]
        dense[pl.ds(at, TILE), pl.ds(to, TILE)] = tile

        @pl.when((far & 1) == 0)
        def _():
            dense_t[pl.ds(to, TILE), pl.ds(inside, TILE)] = tile.T

        @pl.when((far & 1) == 1)
        def _():
            other_t[pl.ds(to, TILE), pl.ds(inside, TILE)] = tile.T

        return carry

    lax.fori_loop(0, count[0, 0], place, 0)


def forward(first, dense, *refs):
    *feats, out = refs
    size = out.shape[0]
    panel = jnp.concatenate([f[...] for f in feats], axis=0)
    out[...] = jnp.dot(
        dense[first : first + size, :], panel, preferred_element_type=F32
    ).astype(out.dtype)


def add_split(mine, other, *outs):
    rows = outs[0].shape[0]
    for k, out in enumerate(outs):
        part = pl.ds(k * rows, rows)
        out[...] = (mine[part, :].astype(F32) + other[part, :].astype(F32)).astype(out.dtype)


def relay(value, out):
    out[...] = value[...]


def add_all(*refs):
    *terms, out = refs
    out[...] = tree([t[...].astype(F32) for t in terms]).astype(out.dtype)


def dense_layer(weight, cotangent, *refs):
    *terms, hidden_out, summed, hidden_grad, grad_rows = refs
    total = tree([t[...].astype(F32) for t in terms]).astype(BF16)
    summed[...] = total
    hidden = jnp.dot(total, weight[...], preferred_element_type=F32)
    hidden_out[...] = hidden
    gate = jax.nn.sigmoid(hidden)
    grad = (cotangent[0].astype(F32) * gate * (1.0 + hidden * (1.0 - gate))).astype(BF16)
    hidden_grad[...] = grad
    grad_rows[...] = lax.dot_general(
        grad, weight[...], (((1,), (1,)), ((), ())), preferred_element_type=F32
    ).astype(BF16)


def activation(hidden, out, done):
    done[...] = jnp.zeros_like(done)
    out[...] = (hidden[...] * jax.nn.sigmoid(hidden[...])).astype(BF16)


def weight_half(n_row, flip, scale, summed, hidden_grad, out, whole):
    me_row, side = lax.axis_index("row"), (lax.axis_index("col") & 1) ^ flip
    half = out.shape[0]
    at = pl.multiple_of(side * half, half)
    whole[...] = (
        lax.dot_general(
            summed[:, pl.ds(at, half)],
            hidden_grad[...],
            (((0,), (0,)), ((), ())),
            preferred_element_type=F32,
        )
        * scale
    )
    piece = half // n_row
    for k in range(n_row):
        rows = pl.ds(pl.multiple_of((me_row ^ k) * piece, piece), piece)
        out[k * piece : (k + 1) * piece, :] = whole[rows, :].astype(out.dtype)


def backward(dense_t, *refs):
    *grads, out = refs
    panel = jnp.concatenate([g[...] for g in grads], axis=0)
    out[...] = jnp.dot(dense_t[...], panel, preferred_element_type=F32).astype(out.dtype)


def messages(mine, other, final_w, own, *outs):
    own[...] = mine[:TILE, :] + other[:TILE, :].astype(F32)
    for k, out in enumerate(outs):
        part = pl.ds((k + 1) * TILE, TILE)
        out[:TILE, :] = (mine[part, :] + other[part, :].astype(F32)).astype(BF16)
        out[TILE:, :] = final_w[...]


def add_rows(own, *refs):
    *terms, out = refs
    total = own[...]
    for t in terms:
        total += t[:TILE, :].astype(F32)
    out[...] = total.astype(BF16)


def join(own, *refs):
    *others, out = refs
    me_row = lax.axis_index("row")
    piece = own.shape[0]
    out[pl.ds(pl.multiple_of(me_row * piece, piece), piece), :] = own[...]
    for k, ref in enumerate(others):
        at = pl.multiple_of((me_row ^ (k + 1)) * piece, piece)
        out[pl.ds(at, piece), :] = ref[TILE:, :]


def spread(mine, other, out):
    core = lax.axis_index("col") & 1
    half = mine.shape[0]
    out[pl.ds(pl.multiple_of(core * half, half), half), :] = mine[...].astype(F32)
    out[pl.ds(pl.multiple_of((1 - core) * half, half), half), :] = other[...].astype(F32)


def local(feats, weight, cotangent, tile_values, tile_rows, tile_cols, tile_count):
    width = feats.shape[2]
    n_row, n_col = lax.axis_size("row"), lax.axis_size("col")
    n_z = n_col // 2
    row_nodes, col_nodes = n_col * TILE, n_row * TILE
    half = row_nodes // 2
    row_swap = lambda x, k: swap(x, "row", n_row, k)
    z_swap = lambda x, k: swap(x, "col", n_col, 2 * k)
    core_swap = lambda x: swap(x, "col", n_col, 1)

    own = feats[0]
    panel = [own] + [row_swap(own, k) for k in range(1, n_row)]
    dense, dense_t, other_t = call(
        functools.partial(densify, n_z),
        [like(row_nodes, col_nodes), like(col_nodes, half), like(col_nodes, half)],
        (tile_values, tile_rows, tile_cols, tile_count),
        specs=[VMEM, SMEM, SMEM, SMEM],
    )
    other_t = core_swap(other_t)
    quarter, parts = half // 2, [None] * n_z
    for odd in (1, 0):
        first = (1 - odd) * quarter
        (other,) = call(
            functools.partial(forward, half + first),
            [like(quarter, width)],
            (dense, *panel),
        )
        other = core_swap(other)
        (mine,) = call(
            functools.partial(forward, first), [like(quarter, width, dtype=F32)], (dense, *panel)
        )
        outs = [like(TILE, width, dtype=BF16 if k else F32) for k in range(odd, n_z, 2)]
        parts[odd::2] = call(add_split, outs, (mine, other))
    bit, extra = 1, []
    while bit < n_z:
        far = [k for k in range(n_z) if k & bit and k % bit == 0]
        for k in sorted(far, reverse=True):
            got = z_swap(parts[k], bit)
            if k == bit:
                extra.append(got)
            else:
                (parts[k ^ bit],) = call(add_all, [like(TILE, width)], (parts[k ^ bit], got))
        bit *= 2
    terms = [parts[0]] + extra
    hidden, summed, hidden_grad, grad_rows = call(
        dense_layer,
        [like(TILE, width, dtype=F32)] + [like(TILE, width)] * 3,
        (weight, cotangent, *terms),
    )
    piece = width // 2 // n_row
    scale = (n_row * n_col * TILE) ** -0.5
    scratch = [pltpu.VMEM((width // 2, width), F32)]
    (other_w,) = call(
        functools.partial(weight_half, n_row, 1, scale),
        [like(width // 2, width)],
        (summed, hidden_grad),
        scratch=scratch,
    )
    other_w = core_swap(other_w)
    (mine_w,) = call(
        functools.partial(weight_half, n_row, 0, scale),
        [like(width // 2, width, dtype=F32)],
        (summed, hidden_grad),
        scratch=scratch,
    )
    parts_w = call(add_split, [like(piece, width)] * n_row, (mine_w, other_w), after=(other_t,))
    terms_w = [parts_w[0]] + [row_swap(parts_w[k], k) for k in range(1, n_row)]
    same = [grad_rows] + [None] * (n_z - 1)
    bit = n_z // 2
    while bit:
        for k in range(0, n_z, 2 * bit):
            same[k | bit] = z_swap(same[k], bit)
            if bit > 1:
                (same[k | bit],) = call(
                    relay, [like(TILE, width)], (same[k | bit],), after=terms_w[1 : n_row - 1]
                )
        bit //= 2
    (plane_w,) = call(add_all, [like(piece, width)], terms_w)
    terms_w = [plane_w] + [z_swap(plane_w, k) for k in range(1, n_z)]
    (final_w,) = call(add_all, [like(piece, width)], terms_w, us=5)
    (other,) = call(backward, [like(col_nodes, width)], (other_t, *same))
    other = core_swap(other)
    (mine,) = call(backward, [like(col_nodes, width, dtype=F32)], (dense_t, *same))
    back, *parts = call(
        messages,
        [like(TILE, width, dtype=F32)] + [like(TILE + piece, width)] * (n_row - 1),
        (mine, other, final_w),
    )
    terms = [row_swap(part, k + 1) for k, part in enumerate(parts)]
    layer_out, done = call(
        activation, [like(TILE, width), like(8, TILE, dtype=F32)], (hidden,), us=1
    )
    (half_w,) = call(join, [like(width // 2, width)], (final_w, *terms), after=(done,))
    other_w = core_swap(half_w)
    (feat_grad,) = call(add_rows, [like(TILE, width)], (back, *terms), after=(half_w,))
    (weight_grad,) = call(spread, [like(width, width, dtype=F32)], (half_w, other_w))
    return layer_out[None], feat_grad[None], weight_grad


def solution(mesh):
    in_specs = (
        P("col", "row", None),
        P(),
        P("row", "col", None),
        P("row", "col", None, None, None),
        P("row", "col", None),
        P("row", "col", None),
        P("row", "col"),
    )
    out_specs = (P("row", "col", None), P("col", "row", None), P())
    return jax.shard_map(local, mesh=mesh, in_specs=in_specs, out_specs=out_specs, check_vma=False)
```

```python
import functools

import jax
import jax.numpy as jnp
from jax import lax
from jax.experimental import pallas as pl
from jax.experimental.pallas import tpu as pltpu
from jax.sharding import PartitionSpec as P

F32 = jnp.float32
BF16 = jnp.bfloat16
VMEM = pl.BlockSpec(memory_space=pltpu.VMEM)
SMEM = pl.BlockSpec(memory_space=pltpu.SMEM)
TILE = 128


def call(kernel, outs, args, specs=None, scratch=(), after=(), us=0):
    held = sum(a.size * a.dtype.itemsize for a in (*args, *outs))

    def body(*refs):
        kernel(*refs[: len(args)], *refs[len(args) + len(after) :])

    return pl.pallas_call(
        body,
        out_shape=outs,
        in_specs=(specs or [VMEM] * len(args)) + [pl.BlockSpec(memory_space=pl.ANY)] * len(after),
        out_specs=[VMEM] * len(outs),
        scratch_shapes=scratch,
        compiler_params=pltpu.CompilerParams(vmem_limit_bytes=12 * 2**20 + 3 * held),
        cost_estimate=pl.CostEstimate(flops=int(us * 1.15e9), bytes_accessed=0, transcendentals=0),
    )(*args, *after)


def like(*shape, dtype=BF16):
    return jax.ShapeDtypeStruct(shape, dtype)


def swap(value, axis, size, mask):
    return lax.ppermute(value, axis, [(i, i ^ mask) for i in range(size)])


def tree(terms):
    while len(terms) > 1:
        terms = [sum(terms[i + 1 : i + 2], terms[i]) for i in range(0, len(terms), 2)]
    return terms[0]


def densify(n_z, values, rows, cols, count, dense, dense_t, other_t):
    me_row, me_col = lax.axis_index("row"), lax.axis_index("col")
    dense[...] = jnp.zeros_like(dense)
    dense_t[...] = jnp.zeros_like(dense_t)
    other_t[...] = jnp.zeros_like(other_t)

    def place(s, carry):
        far = rows[0, 0, s] ^ me_col
        inside = pl.multiple_of((far >> 1) * TILE, TILE)
        chip = far >> 1
        part = (far & 1) * n_z + (1 - (chip & 1)) * (n_z // 2) + (chip >> 1)
        at = pl.multiple_of(part * TILE, TILE)
        to = pl.multiple_of((cols[0, 0, s] ^ me_row) * TILE, TILE)
        tile = values[0, 0, s]
        dense[pl.ds(at, TILE), pl.ds(to, TILE)] = tile

        @pl.when((far & 1) == 0)
        def _():
            dense_t[pl.ds(to, TILE), pl.ds(inside, TILE)] = tile.T

        @pl.when((far & 1) == 1)
        def _():
            other_t[pl.ds(to, TILE), pl.ds(inside, TILE)] = tile.T

        return carry

    lax.fori_loop(0, count[0, 0], place, 0)


def forward(first, dense, *refs):
    *feats, out = refs
    size = out.shape[0]
    panel = jnp.concatenate([f[...] for f in feats], axis=0)
    out[...] = jnp.dot(
        dense[first : first + size, :], panel, preferred_element_type=F32
    ).astype(out.dtype)


def add_split(mine, other, *outs):
    rows = outs[0].shape[0]
    for k, out in enumerate(outs):
        part = pl.ds(k * rows, rows)
        out[...] = (mine[part, :].astype(F32) + other[part, :].astype(F32)).astype(out.dtype)


def relay(value, out):
    out[...] = value[...]


def add_all(*refs):
    *terms, out = refs
    out[...] = tree([t[...].astype(F32) for t in terms]).astype(out.dtype)


def dense_layer(weight, cotangent, *refs):
    *terms, hidden_out, summed, hidden_grad, grad_rows = refs
    total = tree([t[...].astype(F32) for t in terms]).astype(BF16)
    summed[...] = total
    hidden = jnp.dot(total, weight[...], preferred_element_type=F32)
    hidden_out[...] = hidden
    gate = jax.nn.sigmoid(hidden)
    grad = (cotangent[0].astype(F32) * gate * (1.0 + hidden * (1.0 - gate))).astype(BF16)
    hidden_grad[...] = grad
    grad_rows[...] = lax.dot_general(
        grad, weight[...], (((1,), (1,)), ((), ())), preferred_element_type=F32
    ).astype(BF16)


def activation(hidden, out, done):
    done[...] = jnp.zeros_like(done)
    out[...] = (hidden[...] * jax.nn.sigmoid(hidden[...])).astype(BF16)


def weight_term(n_row, scale, summed, hidden_grad, mine, other, whole):
    whole[...] = (
        lax.dot_general(
            summed[...], hidden_grad[...], (((0,), (0,)), ((), ())), preferred_element_type=F32
        )
        * scale
    )
    me_row, core = lax.axis_index("row"), lax.axis_index("col") & 1
    half = mine.shape[0]
    piece = half // n_row
    for k in range(n_row):
        inside = (me_row ^ k) * piece
        part = pl.ds(k * piece, piece)
        at = pl.multiple_of(core * half + inside, piece)
        mine[part, :] = whole[pl.ds(at, piece), :]
        at = pl.multiple_of((1 - core) * half + inside, piece)
        other[part, :] = whole[pl.ds(at, piece), :].astype(BF16)


def backward(dense_t, *refs):
    *grads, out = refs
    panel = jnp.concatenate([g[...] for g in grads], axis=0)
    out[...] = jnp.dot(dense_t[...], panel, preferred_element_type=F32).astype(out.dtype)


def messages(mine, other, final_w, own, *outs):
    own[...] = mine[:TILE, :] + other[:TILE, :].astype(F32)
    for k, out in enumerate(outs):
        part = pl.ds((k + 1) * TILE, TILE)
        out[:TILE, :] = (mine[part, :] + other[part, :].astype(F32)).astype(BF16)
        out[TILE:, :] = final_w[...]


def add_rows(own, *refs):
    *terms, out = refs
    total = own[...]
    for t in terms:
        total += t[:TILE, :].astype(F32)
    out[...] = total.astype(BF16)


def join(own, *refs):
    *others, out = refs
    me_row = lax.axis_index("row")
    piece = own.shape[0]
    out[pl.ds(pl.multiple_of(me_row * piece, piece), piece), :] = own[...]
    for k, ref in enumerate(others):
        at = pl.multiple_of((me_row ^ (k + 1)) * piece, piece)
        out[pl.ds(at, piece), :] = ref[TILE:, :]


def spread(mine, other, out):
    core = lax.axis_index("col") & 1
    half = mine.shape[0]
    out[pl.ds(pl.multiple_of(core * half, half), half), :] = mine[...].astype(F32)
    out[pl.ds(pl.multiple_of((1 - core) * half, half), half), :] = other[...].astype(F32)


def local(feats, weight, cotangent, tile_values, tile_rows, tile_cols, tile_count):
    width = feats.shape[2]
    n_row, n_col = lax.axis_size("row"), lax.axis_size("col")
    n_z = n_col // 2
    row_nodes, col_nodes = n_col * TILE, n_row * TILE
    half = row_nodes // 2
    row_swap = lambda x, k: swap(x, "row", n_row, k)
    z_swap = lambda x, k: swap(x, "col", n_col, 2 * k)
    core_swap = lambda x: swap(x, "col", n_col, 1)

    own = feats[0]
    panel = [own] + [row_swap(own, k) for k in range(1, n_row)]
    dense, dense_t, other_t = call(
        functools.partial(densify, n_z),
        [like(row_nodes, col_nodes), like(col_nodes, half), like(col_nodes, half)],
        (tile_values, tile_rows, tile_cols, tile_count),
        specs=[VMEM, SMEM, SMEM, SMEM],
    )
    other_t = core_swap(other_t)
    quarter, parts = half // 2, [None] * n_z
    for odd in (1, 0):
        first = (1 - odd) * quarter
        (other,) = call(
            functools.partial(forward, half + first),
            [like(quarter, width)],
            (dense, *panel),
        )
        other = core_swap(other)
        (mine,) = call(
            functools.partial(forward, first), [like(quarter, width, dtype=F32)], (dense, *panel)
        )
        outs = [like(TILE, width, dtype=BF16 if k else F32) for k in range(odd, n_z, 2)]
        parts[odd::2] = call(add_split, outs, (mine, other))
    bit, extra = 1, []
    while bit < n_z:
        far = [k for k in range(n_z) if k & bit and k % bit == 0]
        for k in sorted(far, reverse=True):
            got = z_swap(parts[k], bit)
            if k == bit:
                extra.append(got)
            else:
                (parts[k ^ bit],) = call(add_all, [like(TILE, width)], (parts[k ^ bit], got))
        bit *= 2
    terms = [parts[0]] + extra
    hidden, summed, hidden_grad, grad_rows = call(
        dense_layer,
        [like(TILE, width, dtype=F32)] + [like(TILE, width)] * 3,
        (weight, cotangent, *terms),
    )
    piece = width // 2 // n_row
    mine_w, other_w = call(
        functools.partial(weight_term, n_row, (n_row * n_col * TILE) ** -0.5),
        [like(width // 2, width, dtype=F32), like(width // 2, width)],
        (summed, hidden_grad),
        scratch=[pltpu.VMEM((width, width), F32)],
    )
    other_w = core_swap(other_w)
    parts_w = call(add_split, [like(piece, width)] * n_row, (mine_w, other_w), after=(other_t,))
    terms_w = [parts_w[0]] + [row_swap(parts_w[k], k) for k in range(1, n_row)]
    same = [grad_rows] + [None] * (n_z - 1)
    bit = n_z // 2
    while bit:
        for k in range(0, n_z, 2 * bit):
            same[k | bit] = z_swap(same[k], bit)
            if bit > 1:
                (same[k | bit],) = call(
                    relay, [like(TILE, width)], (same[k | bit],), us=3
                )
        bit //= 2
    (plane_w,) = call(add_all, [like(piece, width)], terms_w, us=1)
    terms_w = [plane_w] + [z_swap(plane_w, k) for k in range(1, n_z)]
    (other,) = call(backward, [like(col_nodes, width)], (other_t, *same))
    other = core_swap(other)
    (mine,) = call(backward, [like(col_nodes, width, dtype=F32)], (dense_t, *same))
    (final_w,) = call(add_all, [like(piece, width)], terms_w, after=(mine,), us=5)
    back, *parts = call(
        messages,
        [like(TILE, width, dtype=F32)] + [like(TILE + piece, width)] * (n_row - 1),
        (mine, other, final_w),
    )
    terms = [row_swap(part, k + 1) for k, part in enumerate(parts)]
    layer_out, done = call(
        activation, [like(TILE, width), like(8, TILE, dtype=F32)], (hidden,), us=1
    )
    (half_w,) = call(join, [like(width // 2, width)], (final_w, *terms), after=(done,))
    other_w = core_swap(half_w)
    (feat_grad,) = call(add_rows, [like(TILE, width)], (back, *terms), after=(half_w,))
    (weight_grad,) = call(spread, [like(width, width, dtype=F32)], (half_w, other_w))
    return layer_out[None], feat_grad[None], weight_grad


def solution(mesh):
    in_specs = (
        P("col", "row", None),
        P(),
        P("row", "col", None),
        P("row", "col", None, None, None),
        P("row", "col", None),
        P("row", "col", None),
        P("row", "col"),
    )
    out_specs = (P("row", "col", None), P("col", "row", None), P())
    return jax.shard_map(local, mesh=mesh, in_specs=in_specs, out_specs=out_specs, check_vma=False)
```

```python
import functools

import jax
import jax.numpy as jnp
from jax import lax
from jax.experimental import pallas as pl
from jax.experimental.pallas import tpu as pltpu
from jax.sharding import PartitionSpec as P

F32 = jnp.float32
BF16 = jnp.bfloat16
VMEM = pl.BlockSpec(memory_space=pltpu.VMEM)
SMEM = pl.BlockSpec(memory_space=pltpu.SMEM)
TILE = 128


def call(kernel, outs, args, specs=None, scratch=(), after=(), us=0):
    held = sum(a.size * a.dtype.itemsize for a in (*args, *outs))

    def body(*refs):
        kernel(*refs[: len(args)], *refs[len(args) + len(after) :])

    return pl.pallas_call(
        body,
        out_shape=outs,
        in_specs=(specs or [VMEM] * len(args)) + [pl.BlockSpec(memory_space=pl.ANY)] * len(after),
        out_specs=[VMEM] * len(outs),
        scratch_shapes=scratch,
        compiler_params=pltpu.CompilerParams(vmem_limit_bytes=12 * 2**20 + 3 * held),
        cost_estimate=pl.CostEstimate(flops=int(us * 1.15e9), bytes_accessed=0, transcendentals=0),
    )(*args, *after)


def like(*shape, dtype=BF16):
    return jax.ShapeDtypeStruct(shape, dtype)


def swap(value, axis, size, mask):
    return lax.ppermute(value, axis, [(i, i ^ mask) for i in range(size)])


def tree(terms):
    while len(terms) > 1:
        terms = [sum(terms[i + 1 : i + 2], terms[i]) for i in range(0, len(terms), 2)]
    return terms[0]


def densify(n_z, values, rows, cols, count, dense, dense_t, other_t):
    me_row, me_col = lax.axis_index("row"), lax.axis_index("col")
    dense[...] = jnp.zeros_like(dense)
    dense_t[...] = jnp.zeros_like(dense_t)
    other_t[...] = jnp.zeros_like(other_t)

    def place(s, carry):
        far = rows[0, 0, s] ^ me_col
        inside = pl.multiple_of((far >> 1) * TILE, TILE)
        chip = far >> 1
        part = (far & 1) * n_z + (1 - (chip & 1)) * (n_z // 2) + (chip >> 1)
        at = pl.multiple_of(part * TILE, TILE)
        to = pl.multiple_of((cols[0, 0, s] ^ me_row) * TILE, TILE)
        tile = values[0, 0, s]
        dense[pl.ds(at, TILE), pl.ds(to, TILE)] = tile

        @pl.when((far & 1) == 0)
        def _():
            dense_t[pl.ds(to, TILE), pl.ds(inside, TILE)] = tile.T

        @pl.when((far & 1) == 1)
        def _():
            other_t[pl.ds(to, TILE), pl.ds(inside, TILE)] = tile.T

        return carry

    lax.fori_loop(0, count[0, 0], place, 0)


def forward(first, dense, *refs):
    *feats, out = refs
    size = out.shape[0]
    panel = jnp.concatenate([f[...] for f in feats], axis=0)
    out[...] = jnp.dot(
        dense[first : first + size, :], panel, preferred_element_type=F32
    ).astype(out.dtype)


def add_split(mine, other, *outs):
    rows = outs[0].shape[0]
    for k, out in enumerate(outs):
        part = pl.ds(k * rows, rows)
        out[...] = (mine[part, :].astype(F32) + other[part, :].astype(F32)).astype(out.dtype)


def relay(value, out):
    out[...] = value[...]


def add_all(*refs):
    *terms, out = refs
    out[...] = tree([t[...].astype(F32) for t in terms]).astype(out.dtype)


def dense_layer(weight, cotangent, *refs):
    *terms, hidden_out, summed, hidden_grad, grad_rows = refs
    total = tree([t[...].astype(F32) for t in terms]).astype(BF16)
    summed[...] = total
    hidden = jnp.dot(total, weight[...], preferred_element_type=F32)
    hidden_out[...] = hidden
    gate = jax.nn.sigmoid(hidden)
    grad = (cotangent[0].astype(F32) * gate * (1.0 + hidden * (1.0 - gate))).astype(BF16)
    hidden_grad[...] = grad
    grad_rows[...] = lax.dot_general(
        grad, weight[...], (((1,), (1,)), ((), ())), preferred_element_type=F32
    ).astype(BF16)


def activation(hidden, out, done):
    done[...] = jnp.zeros_like(done)
    out[...] = (hidden[...] * jax.nn.sigmoid(hidden[...])).astype(BF16)


def weight_term(n_row, scale, summed, hidden_grad, mine, other, whole):
    whole[...] = (
        lax.dot_general(
            summed[...], hidden_grad[...], (((0,), (0,)), ((), ())), preferred_element_type=F32
        )
        * scale
    )
    me_row, core = lax.axis_index("row"), lax.axis_index("col") & 1
    half = mine.shape[0]
    piece = half // n_row
    for k in range(n_row):
        inside = (me_row ^ k) * piece
        part = pl.ds(k * piece, piece)
        at = pl.multiple_of(core * half + inside, piece)
        mine[part, :] = whole[pl.ds(at, piece), :]
        at = pl.multiple_of((1 - core) * half + inside, piece)
        other[part, :] = whole[pl.ds(at, piece), :].astype(BF16)


def backward(dense_t, *refs):
    *grads, out = refs
    panel = jnp.concatenate([g[...] for g in grads], axis=0)
    out[...] = jnp.dot(dense_t[...], panel, preferred_element_type=F32).astype(out.dtype)


def messages(mine, other, final_w, own, *outs):
    own[...] = mine[:TILE, :] + other[:TILE, :].astype(F32)
    for k, out in enumerate(outs):
        part = pl.ds((k + 1) * TILE, TILE)
        out[:TILE, :] = (mine[part, :] + other[part, :].astype(F32)).astype(BF16)
        out[TILE:, :] = final_w[...]


def add_rows(own, *refs):
    *terms, out = refs
    total = own[...]
    for t in terms:
        total += t[:TILE, :].astype(F32)
    out[...] = total.astype(BF16)


def join(*refs):
    *pieces, out = refs
    rows = out.shape[0] // len(pieces)
    for k, ref in enumerate(pieces):
        skip = ref.shape[0] - rows
        out[k * rows : (k + 1) * rows, :] = ref[skip:, :]


def spread(*refs):
    *parts, out = refs
    me_row, core = lax.axis_index("row"), lax.axis_index("col") & 1
    n_row = lax.axis_size("row")
    rows = out.shape[0] // 2 // n_row
    for part, ref in enumerate(parts):
        for k in range(n_row // 2):
            place = (core ^ (part // 2)) * n_row + (me_row ^ (part % 2 * (n_row // 2) + k))
            at = pl.multiple_of(place * rows, rows)
            out[pl.ds(at, rows), :] = ref[k * rows : (k + 1) * rows, :].astype(F32)


def local(feats, weight, cotangent, tile_values, tile_rows, tile_cols, tile_count):
    width = feats.shape[2]
    n_row, n_col = lax.axis_size("row"), lax.axis_size("col")
    n_z = n_col // 2
    row_nodes, col_nodes = n_col * TILE, n_row * TILE
    half = row_nodes // 2
    row_swap = lambda x, k: swap(x, "row", n_row, k)
    z_swap = lambda x, k: swap(x, "col", n_col, 2 * k)
    core_swap = lambda x: swap(x, "col", n_col, 1)

    own = feats[0]
    panel = [own] + [row_swap(own, k) for k in range(1, n_row)]
    dense, dense_t, other_t = call(
        functools.partial(densify, n_z),
        [like(row_nodes, col_nodes), like(col_nodes, half), like(col_nodes, half)],
        (tile_values, tile_rows, tile_cols, tile_count),
        specs=[VMEM, SMEM, SMEM, SMEM],
    )
    other_t = core_swap(other_t)
    quarter, parts = half // 2, [None] * n_z
    for odd in (1, 0):
        first = (1 - odd) * quarter
        (other,) = call(
            functools.partial(forward, half + first),
            [like(quarter, width)],
            (dense, *panel),
        )
        other = core_swap(other)
        (mine,) = call(
            functools.partial(forward, first), [like(quarter, width, dtype=F32)], (dense, *panel)
        )
        outs = [like(TILE, width, dtype=BF16 if k else F32) for k in range(odd, n_z, 2)]
        parts[odd::2] = call(add_split, outs, (mine, other))
    bit, extra = 1, []
    while bit < n_z:
        far = [k for k in range(n_z) if k & bit and k % bit == 0]
        for k in sorted(far, reverse=True):
            got = z_swap(parts[k], bit)
            if k == bit:
                extra.append(got)
            else:
                (parts[k ^ bit],) = call(add_all, [like(TILE, width)], (parts[k ^ bit], got))
        bit *= 2
    terms = [parts[0]] + extra
    hidden, summed, hidden_grad, grad_rows = call(
        dense_layer,
        [like(TILE, width, dtype=F32)] + [like(TILE, width)] * 3,
        (weight, cotangent, *terms),
    )
    piece = width // 2 // n_row
    mine_w, other_w = call(
        functools.partial(weight_term, n_row, (n_row * n_col * TILE) ** -0.5),
        [like(width // 2, width, dtype=F32), like(width // 2, width)],
        (summed, hidden_grad),
        scratch=[pltpu.VMEM((width, width), F32)],
    )
    other_w = core_swap(other_w)
    parts_w = call(add_split, [like(piece, width)] * n_row, (mine_w, other_w), after=(other_t,))
    terms_w = [parts_w[0]] + [row_swap(parts_w[k], k) for k in range(1, n_row)]
    same = [grad_rows] + [None] * (n_z - 1)
    bit = n_z // 2
    while bit:
        for k in range(0, n_z, 2 * bit):
            same[k | bit] = z_swap(same[k], bit)
            if bit > 1:
                (same[k | bit],) = call(
                    relay, [like(TILE, width)], (same[k | bit],), us=3
                )
        bit //= 2
    (plane_w,) = call(add_all, [like(piece, width)], terms_w, us=1)
    terms_w = [plane_w] + [z_swap(plane_w, k) for k in range(1, n_z)]
    (other,) = call(backward, [like(col_nodes, width)], (other_t, *same))
    other = core_swap(other)
    (mine,) = call(backward, [like(col_nodes, width, dtype=F32)], (dense_t, *same))
    (final_w,) = call(add_all, [like(piece, width)], terms_w, after=(mine,), us=5)
    back, *parts = call(
        messages,
        [like(TILE, width, dtype=F32)] + [like(TILE + piece, width)] * (n_row - 1),
        (mine, other, final_w),
    )
    terms = [row_swap(part, k + 1) for k, part in enumerate(parts)]
    layer_out, done = call(
        activation, [like(TILE, width), like(8, TILE, dtype=F32)], (hidden,), us=1
    )
    half_row = n_row // 2
    early = [final_w] + [t for t in terms[: half_row - 1]]
    (early_w,) = call(join, [like(half_row * piece, width)], early, after=(done,))
    early_other = core_swap(early_w)
    (late_w,) = call(join, [like(half_row * piece, width)], terms[half_row - 1 :], after=(early_other,))
    late_other = core_swap(late_w)
    (feat_grad,) = call(add_rows, [like(TILE, width)], (back, *terms), after=(late_w,))
    (weight_grad,) = call(
        spread, [like(width, width, dtype=F32)], (early_w, late_w, early_other, late_other)
    )
    return layer_out[None], feat_grad[None], weight_grad


def solution(mesh):
    in_specs = (
        P("col", "row", None),
        P(),
        P("row", "col", None),
        P("row", "col", None, None, None),
        P("row", "col", None),
        P("row", "col", None),
        P("row", "col"),
    )
    out_specs = (P("row", "col", None), P("col", "row", None), P())
    return jax.shard_map(local, mesh=mesh, in_specs=in_specs, out_specs=out_specs, check_vma=False)
```
